32 devices in a mesh: band: 2 (over core), dom: 16 (over z, y, x).
Axes of the slice: x: 2, y: 2, z: 4, core: 2. Of those that a mesh axis runs over, the one named last changes fastest.
Arguments:
- orbitals: float32 [24, 32, 128, 128], P('band', 'dom'), may hold values from -6 to 6
- occupations: float32 [24], replicated, may hold values from 0.25 to 2
Outputs:
- exchange_terms: float32 [24, 32, 128, 128], P('band', 'dom')
The draws below stay inside these ranges and needn't reach their ends.
All inputs are finite; a program needn't handle non-finite values.
Results may differ from the reference program's by a relative error of at most 0.0001.
Values sent between devices are 32-bit elements; how exact they have to be, the bound alone decides.
No kernel may reach another device: no remote copies, remote signals or barrier semaphores. Data moves between devices by JAX's collectives and lax.ppermute only.
A program may use at most 128 MiB of HBM per device.

```python
import math
import jax
import jax.numpy as jnp
from jax import lax

ORB_DEV = 12
BLOCK = 2
STEPS = 2
SWEEPS = 2
CY = 128
CZ = 128
NORB = 24
NX = 32
N_BAND = 2


def draw_orbitals(key, part):
    first_key = jax.random.fold_in(key, 0)
    rough_part = jnp.clip(jax.random.normal(first_key, (NORB, NX, CY, CZ), jnp.float32), -4.0, 4.0)
    return rough_part


def setup_inputs(seed: int = 0) -> dict:
    keys = jax.random.split(jax.random.key(seed), 3)
    orbitals = draw_orbitals(jax.random.fold_in(keys[2], 71), 0)
    occupations = jnp.clip(jnp.exp(jax.random.uniform(keys[1], (NORB,), jnp.float32, math.log(0.25), math.log(2.0))), 0.25, 2.0)
    return dict(orbitals=orbitals, occupations=occupations)


def neighbours(field):
    lead = field.ndim - 3
    padded = jnp.pad(field, [(0, 0)] * lead + [(1, 1)] * 3)
    total = padded[..., 2:, 1:-1, 1:-1] + padded[..., :-2, 1:-1, 1:-1]
    total = total + padded[..., 1:-1, 2:, 1:-1] + padded[..., 1:-1, :-2, 1:-1]
    total = total + padded[..., 1:-1, 1:-1, 2:] + padded[..., 1:-1, 1:-1, :-2]
    return total


def solve_potential(density):
    potential = density / 6.0
    for sweep_index in range(SWEEPS):
        potential = (density + neighbours(potential)) / 6.0
    return potential


def reference(orbitals, occupations):
    exchange_terms = jnp.zeros(orbitals.shape, jnp.float32)
    for step_index in range(STEPS):
        owner = step_index * (N_BAND // STEPS)
        first = owner * ORB_DEV + step_index * BLOCK
        owner_block = orbitals[first:first + BLOCK]
        weights = occupations[first:first + BLOCK]

        def per_orbital(target):
            density = owner_block * target[None]
            potential = solve_potential(density)
            step_sum = jnp.zeros(target.shape, jnp.float32)
            for block_index in range(BLOCK):
                step_sum = step_sum - weights[block_index] * potential[block_index] * owner_block[block_index]
            return step_sum

        exchange_terms = exchange_terms + lax.map(per_orbital, orbitals)
    return exchange_terms
```

```python
import functools

import jax
import jax.numpy as jnp
from jax import lax
from jax.experimental import pallas as pl
from jax.experimental.pallas import tpu as pltpu
from jax.sharding import PartitionSpec as P

BLOCK = 2
STEPS = 2
CHUNKS = (3, 3, 3, 3)

ONE = 1.0 / 36.0
TWO = 1.0 / 216.0
CROSS = 2.0 / 216.0

OWN = [(0, 0), (1, 0), (-1, 0), (2, 0), (-2, 0), (0, 1), (1, 1), (-1, 1), (0, -1), (1, -1), (-1, -1), (0, 2), (0, -2)]
BESIDE = [(0, 0), (1, 0), (-1, 0), (0, 1), (0, -1)]


def shifted(field, dy, dz):
    rows, columns = field.shape
    if dy:
        field = pltpu.roll(field, (-dy) % rows, 0)
    if dz:
        field = pltpu.roll(field, (-dz) % columns, 1)
    return field


def inside(shape, dy, dz):
    y = lax.broadcasted_iota(jnp.int32, shape, 0) + dy
    z = lax.broadcasted_iota(jnp.int32, shape, 1) - dz
    return (y >= 0) & (y < shape[0]) & (z >= 0) & (z < shape[1])


def pair_weight(weights, here, there, dy, dz, scale):
    total = None
    for w, h, t in zip(weights, here, there):
        term = (w * shifted(h, 0, -dz)) * shifted(t, dy, 0)
        total = term if total is None else total + term
    total = total * (-scale)
    if dy or dz:
        total = jnp.where(inside(total.shape, dy, dz), total, 0.0)
    return total


def scale_of(dy, dz, dx):
    length = abs(dx) + abs(dy) + abs(dz)
    if length == 1:
        return ONE
    return TWO if max(abs(dx), abs(dy), abs(dz)) == 2 else CROSS


def block_weights(occ_ref, orb_count, swapped):
    groups = lax.axis_size("band")
    out = []
    for step in range(STEPS):
        if swapped:
            s = lax.rem(lax.axis_index("band") + step, STEPS)
        else:
            s = step
        first = s * (groups // STEPS) * orb_count + s * BLOCK
        out += [occ_ref[first + i] for i in range(BLOCK)]
    return out


def local_kernel(swapped, occ_ref, orb_ref, *refs):
    block_refs, acc_ref, k_ref = refs[:STEPS], refs[STEPS], refs[STEPS + 1]
    orb_count, planes, rows, columns = orb_ref.shape
    weights = block_weights(occ_ref, orb_count, swapped)
    dom, slabs = lax.axis_index("dom"), lax.axis_size("dom")
    for p in range(planes):
        here = [r[i, p] for r in block_refs for i in range(BLOCK)]
        there = [r[i, 1 - p] for r in block_refs for i in range(BLOCK)]
        outer = jnp.where(dom == (0 if p == 0 else slabs - 1), 0.0, 1.0)
        y = lax.broadcasted_iota(jnp.int32, (rows, columns), 0)
        z = lax.broadcasted_iota(jnp.int32, (rows, columns), 1)
        edges = (y > 0).astype(jnp.float32) + (y < rows - 1).astype(jnp.float32)
        edges = edges + (z > 0).astype(jnp.float32) + (z < columns - 1).astype(jnp.float32)
        centre = 1.0 / 6.0 + (edges + (1.0 + outer)) * TWO
        for k, (dy, dz) in enumerate(OWN):
            if k == 0:
                k_ref[p, k] = pair_weight(weights, here, here, 0, 0, 1.0) * centre
            else:
                k_ref[p, k] = pair_weight(weights, here, here, dy, dz, scale_of(dy, dz, 0))
        for k, (dy, dz) in enumerate(BESIDE):
            k_ref[p, len(OWN) + k] = pair_weight(weights, here, there, dy, dz, scale_of(dy, dz, 1))

    @pl.loop(0, orb_count)
    def _(j):
        for p in range(planes):
            groups = {}
            for plane, terms, base in ((p, OWN, 0), (1 - p, BESIDE, len(OWN))):
                field = orb_ref[j, plane]
                for k, (dy, dz) in enumerate(terms):
                    term = k_ref[p, base + k] * shifted(field, dy, 0)
                    groups[dz] = groups[dz] + term if dz in groups else term
            out = groups[0]
            for dz in (1, -1, 2, -2):
                out = out + shifted(groups[dz], 0, dz)
            acc_ref[j, p] = out


def sides():
    odd = lax.rem(lax.axis_index("dom"), 2)
    return odd, 1 - odd


def halo_weight_kernel(swapped, orb_count, occ_ref, *refs):
    n = STEPS
    local, first, second, k_ref = refs[:n], refs[n : 2 * n], refs[2 * n : 3 * n], refs[3 * n]
    weights = block_weights(occ_ref, orb_count, swapped)
    for h, (slab, near) in enumerate(zip((first, second), sides())):
        far = 1 - near
        here = [r[i, far] for r in local for i in range(BLOCK)]
        behind = [r[i, near] for r in local for i in range(BLOCK)]
        there = [r[i, near] for r in slab for i in range(BLOCK)]
        beyond = [r[i, far] for r in slab for i in range(BLOCK)]
        for k, (dy, dz) in enumerate(BESIDE):
            k_ref[h, k] = pair_weight(weights, here, there, dy, dz, scale_of(dy, dz, 1))
        k_ref[h, 5] = pair_weight(weights, here, beyond, 0, 0, TWO)
        k_ref[h, 6] = pair_weight(weights, behind, there, 0, 0, TWO)


def halo_kernel(k_ref, first_ref, second_ref, acc_ref, out_ref):
    @pl.loop(0, acc_ref.shape[0])
    def _(j):
        out_ref[j] = acc_ref[j]
        for h, (slab, near) in enumerate(zip((first_ref, second_ref), sides())):
            far = 1 - near
            there = slab[j, near]
            groups = {}
            for k, (dy, dz) in enumerate(BESIDE):
                term = k_ref[h, k] * shifted(there, dy, 0)
                groups[dz] = groups[dz] + term if dz in groups else term
            total = groups[0] + k_ref[h, 5] * slab[j, far]
            total = total + shifted(groups[1], 0, 1) + shifted(groups[-1], 0, -1)
            out_ref[j, far] += total
            out_ref[j, near] += k_ref[h, 6] * there


VMEM = pl.BlockSpec(memory_space=pltpu.VMEM)
SMEM = pl.BlockSpec(memory_space=pltpu.SMEM)
PARAMS = pltpu.CompilerParams(vmem_limit_bytes=32 * 1024 * 1024)


def hops(slabs):
    swap = [(i, i ^ 1) for i in range(slabs)]
    onward = [(i, i + 2 if i % 2 == 0 else i - 2) for i in range(slabs)]
    onward = [(a, b) for a, b in onward if 0 <= b < slabs]
    return swap, onward


def everywhere(field, groups):
    band = lax.axis_index("band")
    if groups == STEPS:
        own = lax.dynamic_slice_in_dim(field, band * BLOCK, BLOCK, 0)
        return [own] + [
            lax.ppermute(own, "band", [(i, (i - step) % STEPS) for i in range(STEPS)]) for step in range(1, STEPS)
        ]
    out = []
    for step in range(STEPS):
        mine = field[step * BLOCK : (step + 1) * BLOCK]
        mine = jnp.where(band == step * (groups // STEPS), mine, jnp.zeros_like(mine))
        out.append(lax.psum(mine, "band"))
    return out


def per_device(orbitals, occupations):
    orb_count, planes, rows, columns = orbitals.shape
    groups, slabs = lax.axis_size("band"), lax.axis_size("dom")
    assert planes == 2 and slabs % 2 == 0 and sum(CHUNKS) == orb_count
    swapped = groups == STEPS
    swap, onward = hops(slabs)

    first, second, start = [], [], 0
    for size in CHUNKS:
        first.append(lax.ppermute(orbitals[start : start + size], "dom", swap))
        start += size
    for slab in first:
        second.append(lax.ppermute(slab, "dom", onward))

    local = everywhere(orbitals[: STEPS * BLOCK], groups)
    acc = pl.pallas_call(
        functools.partial(local_kernel, swapped),
        out_shape=jax.ShapeDtypeStruct(orbitals.shape, jnp.float32),
        in_specs=[SMEM] + [VMEM] * (1 + STEPS),
        out_specs=VMEM,
        scratch_shapes=[pltpu.VMEM((planes, len(OWN) + len(BESIDE), rows, columns), jnp.float32)],
        compiler_params=PARAMS,
        cost_estimate=pl.CostEstimate(flops=50_000_000, bytes_accessed=4_000_000, transcendentals=0),
        name="local",
    )(occupations, orbitals, *local)

    count = 0
    while sum(CHUNKS[:count]) < STEPS * BLOCK:
        count += 1
    near = [everywhere(jnp.concatenate(part[:count])[: STEPS * BLOCK], groups) for part in (first, second)]
    weights = pl.pallas_call(
        functools.partial(halo_weight_kernel, swapped, orb_count),
        out_shape=jax.ShapeDtypeStruct((2, 7, rows, columns), jnp.float32),
        in_specs=[SMEM] + [VMEM] * (3 * STEPS),
        out_specs=VMEM,
        compiler_params=PARAMS,
        name="halo_weights",
    )(occupations, *local, *near[0], *near[1])

    start = 0
    for slab_a, slab_b in zip(first, second):
        size = slab_a.shape[0]
        index = start // size
        spec = pl.BlockSpec((size, planes, rows, columns), lambda i, index=index: (index, 0, 0, 0))
        whole = lambda a: pl.BlockSpec(a.shape, lambda i, n=a.ndim: (0,) * n)
        acc = pl.pallas_call(
            halo_kernel,
            grid=(1,),
            out_shape=jax.ShapeDtypeStruct(orbitals.shape, jnp.float32),
            in_specs=[whole(weights), whole(slab_a), whole(slab_b), spec],
            out_specs=spec,
            input_output_aliases={3: 0},
            compiler_params=PARAMS,
            name="halo",
        )(weights, slab_a, slab_b, acc)
        start += size
    return acc


def solution(mesh):
    in_specs = (P("band", "dom", None, None), P())
    out_specs = P("band", "dom", None, None)
    return jax.shard_map(
        per_device, mesh=mesh, in_specs=in_specs, out_specs=out_specs, check_vma=False
    )
```

```python
import functools

import jax
import jax.numpy as jnp
from jax import lax
from jax.experimental import pallas as pl
from jax.experimental.pallas import tpu as pltpu
from jax.sharding import PartitionSpec as P

BLOCK = 2
STEPS = 2
PLANES = 2
CHUNKS = (5, 4, 5, 5, 5)

ONE = 1.0 / 36.0
TWO = 1.0 / 216.0
CROSS = 2.0 / 216.0

OWN = [(0, 0), (1, 0), (-1, 0), (2, 0), (-2, 0), (0, 1), (1, 1), (-1, 1), (0, -1), (1, -1), (-1, -1), (0, 2), (0, -2)]
BESIDE = [(0, 0), (1, 0), (-1, 0), (0, 1), (0, -1)]
BEYOND, ACROSS = len(BESIDE), len(BESIDE) + 1


def shifted(field, dy, dz):
    rows, columns = field.shape
    if dy:
        field = pltpu.roll(field, (-dy) % rows, 0)
    if dz:
        field = pltpu.roll(field, (-dz) % columns, 1)
    return field


def inside(shape, dy, dz):
    y = lax.broadcasted_iota(jnp.int32, shape, 0) + dy
    z = lax.broadcasted_iota(jnp.int32, shape, 1) - dz
    return (y >= 0) & (y < shape[0]) & (z >= 0) & (z < shape[1])


def pair_weight(here, there, dy, dz, scale):
    total = None
    for h, t in zip(here, there):
        term = shifted(h, 0, -dz) * shifted(t, dy, 0)
        total = term if total is None else total + term
    total = total * (-scale)
    if dy or dz:
        total = jnp.where(inside(total.shape, dy, dz), total, 0.0)
    return total


def scale_of(dy, dz, dx):
    length = abs(dx) + abs(dy) + abs(dz)
    if length == 1:
        return ONE
    return TWO if max(abs(dx), abs(dy), abs(dz)) == 2 else CROSS


def block_weights(occ_ref, orb_count):
    groups = lax.axis_size("band")
    out = []
    for step in range(STEPS):
        s = lax.rem(lax.axis_index("band") + step, STEPS) if groups == STEPS else step
        first = s * (groups // STEPS) * orb_count + s * BLOCK
        out += [occ_ref[first + i] for i in range(BLOCK)]
    return out


def local_weight_kernel(orb_count, occ_ref, *refs):
    block_refs, k_ref = refs[:STEPS], refs[STEPS]
    rows, columns = k_ref.shape[2:]
    weights = block_weights(occ_ref, orb_count)
    dom, slabs = lax.axis_index("dom"), lax.axis_size("dom")
    for p in range(PLANES):
        here = [r[i, p] for r in block_refs for i in range(BLOCK)]
        there = [r[i, 1 - p] for r in block_refs for i in range(BLOCK)]
        weighted = [w * h for w, h in zip(weights, here)]
        outer = jnp.where(dom == (0 if p == 0 else slabs - 1), 0.0, 1.0)
        y = lax.broadcasted_iota(jnp.int32, (rows, columns), 0)
        z = lax.broadcasted_iota(jnp.int32, (rows, columns), 1)
        edges = (y > 0).astype(jnp.float32) + (y < rows - 1).astype(jnp.float32)
        edges = edges + (z > 0).astype(jnp.float32) + (z < columns - 1).astype(jnp.float32)
        centre = 1.0 / 6.0 + (edges + (1.0 + outer)) * TWO
        for k, (dy, dz) in enumerate(OWN):
            if k == 0:
                k_ref[p, k] = pair_weight(weighted, here, 0, 0, 1.0) * centre
            else:
                k_ref[p, k] = pair_weight(weighted, here, dy, dz, scale_of(dy, dz, 0))
        for k, (dy, dz) in enumerate(BESIDE):
            k_ref[p, len(OWN) + k] = pair_weight(weighted, there, dy, dz, scale_of(dy, dz, 1))


def local_kernel(k_ref, orb_ref, *acc_refs):
    base = 0
    for acc_ref in acc_refs:

        @pl.loop(0, acc_ref.shape[0])
        def _(j, acc_ref=acc_ref, base=base):
            for p in range(PLANES):
                groups = {}
                for plane, terms, first in ((p, OWN, 0), (1 - p, BESIDE, len(OWN))):
                    field = orb_ref[base + j, plane]
                    for k, (dy, dz) in enumerate(terms):
                        term = k_ref[p, first + k] * shifted(field, dy, 0)
                        groups[dz] = groups[dz] + term if dz in groups else term
                out = groups[0]
                for dz in (1, -1, 2, -2):
                    out = out + shifted(groups[dz], 0, dz)
                acc_ref[j, p] = out

        base += acc_ref.shape[0]


def nearest():
    odd = lax.rem(lax.axis_index("dom"), 2)
    return odd, 1 - odd


def halo_weight_kernel(orb_count, occ_ref, *refs):
    n = STEPS
    local, slabs = refs[:n], refs[n : 3 * n]
    k_refs = refs[3 * n :]
    weights = block_weights(occ_ref, orb_count)
    dom, count = lax.axis_index("dom"), lax.axis_size("dom")
    real = (1.0, jnp.where((dom == 0) | (dom == count - 1), 0.0, 1.0))
    for h, near in enumerate(nearest()):
        far = 1 - near
        here = [w * r[i, far] for w, (r, i) in zip(weights, [(r, i) for r in local for i in range(BLOCK)])]
        behind = [w * r[i, near] for w, (r, i) in zip(weights, [(r, i) for r in local for i in range(BLOCK)])]
        there = [r[i, near] for r in slabs[h::2] for i in range(BLOCK)]
        beyond = [r[i, far] for r in slabs[h::2] for i in range(BLOCK)]
        for k, (dy, dz) in enumerate(BESIDE):
            k_refs[h][k] = pair_weight(here, there, dy, dz, scale_of(dy, dz, 1) * real[h])
        k_refs[h][BEYOND] = pair_weight(here, beyond, 0, 0, TWO * real[h])
        k_refs[h][ACROSS] = pair_weight(behind, there, 0, 0, TWO * real[h])


def add_near(out_ref, j, k_ref, plane, near):
    groups = {}
    for k, (dy, dz) in enumerate(BESIDE):
        term = k_ref[k] * shifted(plane, dy, 0)
        groups[dz] = groups[dz] + term if dz in groups else term
    out_ref[j, 1 - near] += groups[0] + shifted(groups[1], 0, 1) + shifted(groups[-1], 0, -1)
    out_ref[j, near] += k_ref[ACROSS] * plane


def add_far(out_ref, j, k_ref, plane, near):
    out_ref[j, 1 - near] += k_ref[BEYOND] * plane


def add_chunk(out_ref, origin, k_ref, chunk_ref, start, near):
    size = chunk_ref.shape[0]
    head = start % PLANES
    full = (size - head) // PLANES
    for at in ([0] if head else []) + ([size - 1] if (size - head) % PLANES else []):
        j, m = (start + at) // PLANES - origin, (start + at) % PLANES

        @pl.when(near == m)
        def _(j=j, at=at):
            add_near(out_ref, j, k_ref, chunk_ref[at], near)

        @pl.when(near != m)
        def _(j=j, at=at):
            add_far(out_ref, j, k_ref, chunk_ref[at], near)

    first = (start + head) // PLANES - origin

    @pl.loop(0, full)
    def _(i):
        at = head + PLANES * i
        add_near(out_ref, first + i, k_ref, chunk_ref[at + near], near)
        add_far(out_ref, first + i, k_ref, chunk_ref[at + 1 - near], near)


def finish_kernel(parts, origin, written, chained, *refs):
    n = len(parts)
    k_refs, chunk_refs, acc_ref = refs[:2], refs[2 : 2 + n], refs[2 + n]
    refs = refs[3 + n + chained :]
    out_ref, refs = refs[0], refs[1:]
    rest = acc_ref.shape[0] - written
    sum_ref, sems = refs[-2:]
    sum_ref[...] = acc_ref[...]
    near = nearest()
    for (hop, start), chunk_ref in zip(parts, chunk_refs):
        add_chunk(sum_ref, origin, k_refs[hop], chunk_ref, start, near[hop])
    copies = [
        pltpu.make_async_copy(sum_ref.at[j], out_ref.at[origin + j], sems.at[j]) for j in range(written)
    ]
    for copy in copies:
        copy.start()
    if rest:
        refs[0][...] = sum_ref[pl.ds(written, rest)]
    for copy in copies:
        copy.wait()


VMEM = pl.BlockSpec(memory_space=pltpu.VMEM)
SMEM = pl.BlockSpec(memory_space=pltpu.SMEM)
ANY = pl.BlockSpec(memory_space=pl.ANY)
PARAMS = pltpu.CompilerParams(vmem_limit_bytes=16 * 1024 * 1024)


def finish(name, parts, origin, written, weights, chunks, acc, out, shape):
    rest = acc.shape[0] - written
    out_shape, out_specs = [jax.ShapeDtypeStruct(shape, jnp.float32)], [ANY]
    if rest:
        out_shape.append(jax.ShapeDtypeStruct((rest, *acc.shape[1:]), jnp.float32))
        out_specs.append(VMEM)
    chained = out is not None
    result = pl.pallas_call(
        functools.partial(finish_kernel, parts, origin, written, chained),
        out_shape=out_shape,
        in_specs=[VMEM] * (3 + len(parts)) + [ANY] * chained,
        out_specs=out_specs,
        input_output_aliases={3 + len(parts): 0} if chained else {},
        scratch_shapes=[pltpu.VMEM(acc.shape, jnp.float32), pltpu.SemaphoreType.DMA((written,))],
        compiler_params=PARAMS,
        cost_estimate=pl.CostEstimate(flops=1, bytes_accessed=1, transcendentals=0),
        name=name,
    )(*weights, *chunks, acc, *([out] if chained else []))
    return result


def hops(slabs):
    swap = [(i, i ^ 1) for i in range(slabs)]
    onward = [(i, i + 2 if i % 2 == 0 else i - 2) for i in range(slabs)]
    ring = [(a, b % slabs) for a, b in onward]
    closed = [(a, b if 0 <= b < slabs else a ^ 1) for a, b in onward]
    return swap, ring, closed


def everywhere(field, groups):
    band, axis = lax.axis_index("band"), field.ndim - 4
    if groups == STEPS:
        own = lax.dynamic_slice_in_dim(field, band * BLOCK, BLOCK, axis)
        with jax.named_scope("band_swap"):
            return [own] + [
                lax.ppermute(own, "band", [(i, (i - step) % STEPS) for i in range(STEPS)]) for step in range(1, STEPS)
            ]
    out = []
    for step in range(STEPS):
        mine = lax.slice_in_dim(field, step * BLOCK, (step + 1) * BLOCK, axis=axis)
        mine = jnp.where(band == step * (groups // STEPS), mine, jnp.zeros_like(mine))
        out.append(lax.psum(mine, "band"))
    return out


def after(value, *others):
    return lax.optimization_barrier((value, *others))[0]


def per_device(orbitals, occupations):
    orb_count, planes, rows, columns = orbitals.shape
    groups, slabs = lax.axis_size("band"), lax.axis_size("dom")
    assert planes == PLANES and slabs % 2 == 0 and slabs > 2 and sum(CHUNKS) == orb_count * planes
    swap, ring, closed = hops(slabs)
    starts = [sum(CHUNKS[:i]) for i in range(len(CHUNKS))]
    cuts = (0, starts[-2] // planes, starts[-1] // planes, orb_count)
    assert starts[-2] % planes == 0
    f32 = lambda *shape: jax.ShapeDtypeStruct(shape, jnp.float32)

    flat = orbitals.reshape(-1, rows, columns)
    head = flat[: CHUNKS[0]]
    sent = [head] + [flat[s : s + n] for s, n in zip(starts[1:], CHUNKS[1:])]
    first = []
    for i, part in enumerate(sent):
        with jax.named_scope(f"hop1_part{i}"):
            first.append(lax.ppermute(part, "dom", swap))

    local = everywhere(orbitals[: STEPS * BLOCK], groups)
    k_local = pl.pallas_call(
        functools.partial(local_weight_kernel, orb_count),
        out_shape=f32(planes, len(OWN) + len(BESIDE), rows, columns),
        in_specs=[SMEM] + [VMEM] * STEPS,
        out_specs=VMEM,
        compiler_params=PARAMS,
        cost_estimate=pl.CostEstimate(flops=1, bytes_accessed=1, transcendentals=0),
        name="local_weights",
    )(occupations, *local)
    acc = pl.pallas_call(
        local_kernel,
        out_shape=[f32(b - a, planes, rows, columns) for a, b in ((0, cuts[1]), (cuts[1], orb_count))],
        in_specs=[VMEM] * 2,
        out_specs=[VMEM] * 2,
        compiler_params=PARAMS,
        cost_estimate=pl.CostEstimate(flops=1, bytes_accessed=1, transcendentals=0),
        name="local",
    )(k_local, orbitals)

    second = []
    for i, part in enumerate(first):
        if i == 1:
            part = after(part, k_local)
        if i == 2:
            part = after(part, acc)
        with jax.named_scope(f"hop2_part{i}"):
            second.append(lax.ppermute(part, "dom", closed if i == len(CHUNKS) - 1 else ring))

    count = 0
    while sum(CHUNKS[:count]) < STEPS * BLOCK * planes:
        count += 1
    near = [
        jnp.concatenate(part[:count])[: STEPS * BLOCK * planes].reshape(-1, planes, rows, columns)
        for part in (first, second)
    ]
    near[0] = after(near[0], second[0])
    near = [x for part in zip(*[everywhere(f, groups) for f in near]) for x in part]
    k_halo = pl.pallas_call(
        functools.partial(halo_weight_kernel, orb_count),
        out_shape=[f32(ACROSS + 1, rows, columns)] * 2,
        in_specs=[SMEM] + [VMEM] * (3 * STEPS),
        out_specs=[VMEM] * 2,
        compiler_params=PARAMS,
        cost_estimate=pl.CostEstimate(flops=1, bytes_accessed=1, transcendentals=0),
        name="halo_weights",
    )(occupations, *local, *near)

    n = len(CHUNKS)
    early = [(hop, i) for i in range(n - 2) for hop in (0, 1)]
    later = [(0, n - 2), (0, n - 1), (1, n - 2)]
    last = [(1, n - 1)]
    out, origin, rest = None, 0, None
    for name, parts, upto in (("early", early, cuts[1]), ("later", later, cuts[2]), ("last", last, orb_count)):
        chunks = [(first, second)[hop][i] for hop, i in parts]
        part_acc = {"early": acc[0], "later": acc[1], "last": rest}[name]
        result = finish(
            name, [(hop, starts[i]) for hop, i in parts], origin, upto - origin, k_halo, chunks, part_acc, out, orbitals.shape
        )
        out, rest = result[0], result[-1]
        origin = upto
    return out


def solution(mesh):
    in_specs = (P("band", "dom", None, None), P())
    out_specs = P("band", "dom", None, None)
    return jax.shard_map(
        per_device, mesh=mesh, in_specs=in_specs, out_specs=out_specs, check_vma=False
    )
```

```python
import functools

import jax
import jax.numpy as jnp
from jax import lax
from jax.experimental import pallas as pl
from jax.experimental.pallas import tpu as pltpu
from jax.sharding import PartitionSpec as P

BLOCK = 2
STEPS = 2
PLANES = 2
CHUNKS = (4, 6, 6, 4, 4)
GROUPS = (3, 5)

ONE = 1.0 / 36.0
TWO = 1.0 / 216.0
CROSS = 2.0 / 216.0

OWN = [(0, 0), (1, 0), (-1, 0), (2, 0), (-2, 0), (0, 1), (1, 1), (-1, 1), (0, -1), (1, -1), (-1, -1), (0, 2), (0, -2)]
BESIDE = [(0, 0), (1, 0), (-1, 0), (0, 1), (0, -1)]
BEYOND, ACROSS = len(BESIDE), len(BESIDE) + 1


def shifted(field, dy, dz):
    rows, columns = field.shape
    if dy:
        field = pltpu.roll(field, (-dy) % rows, 0)
    if dz:
        field = pltpu.roll(field, (-dz) % columns, 1)
    return field


def inside(shape, dy, dz):
    y = lax.broadcasted_iota(jnp.int32, shape, 0) + dy
    z = lax.broadcasted_iota(jnp.int32, shape, 1) - dz
    return (y >= 0) & (y < shape[0]) & (z >= 0) & (z < shape[1])


def pair_weight(here, there, dy, dz, scale):
    total = None
    for h, t in zip(here, there):
        term = shifted(h, 0, -dz) * shifted(t, dy, 0)
        total = term if total is None else total + term
    total = total * (-scale)
    if dy or dz:
        total = jnp.where(inside(total.shape, dy, dz), total, 0.0)
    return total


def scale_of(dy, dz, dx):
    length = abs(dx) + abs(dy) + abs(dz)
    if length == 1:
        return ONE
    return TWO if max(abs(dx), abs(dy), abs(dz)) == 2 else CROSS


def block_weights(occ_ref, orb_count):
    groups = lax.axis_size("band")
    out = []
    for step in range(STEPS):
        s = lax.rem(lax.axis_index("band") + step, STEPS) if groups == STEPS else step
        first = s * (groups // STEPS) * orb_count + s * BLOCK
        out += [occ_ref[first + i] for i in range(BLOCK)]
    return out


def cut_kernel(starts, orb_ref, *refs):
    part_refs, sems = refs[:-1], refs[-1]
    flat = orb_ref.reshape(-1, *orb_ref.shape[2:])
    copies = [
        pltpu.make_async_copy(flat.at[pl.ds(start, part.shape[0])], part, sems.at[i])
        for i, (start, part) in enumerate(zip(starts, part_refs))
    ]
    for copy in copies:
        copy.start()
    for copy in copies:
        copy.wait()


def local_weight_kernel(orb_count, occ_ref, *refs):
    block_refs, k_ref = refs[:STEPS], refs[STEPS]
    rows, columns = k_ref.shape[2:]
    weights = block_weights(occ_ref, orb_count)
    dom, slabs = lax.axis_index("dom"), lax.axis_size("dom")
    for p in range(PLANES):
        here = [r[i, p] for r in block_refs for i in range(BLOCK)]
        there = [r[i, 1 - p] for r in block_refs for i in range(BLOCK)]
        weighted = [w * h for w, h in zip(weights, here)]
        outer = jnp.where(dom == (0 if p == 0 else slabs - 1), 0.0, 1.0)
        y = lax.broadcasted_iota(jnp.int32, (rows, columns), 0)
        z = lax.broadcasted_iota(jnp.int32, (rows, columns), 1)
        edges = (y > 0).astype(jnp.float32) + (y < rows - 1).astype(jnp.float32)
        edges = edges + (z > 0).astype(jnp.float32) + (z < columns - 1).astype(jnp.float32)
        centre = 1.0 / 6.0 + (edges + (1.0 + outer)) * TWO
        for k, (dy, dz) in enumerate(OWN):
            if k == 0:
                k_ref[p, k] = pair_weight(weighted, here, 0, 0, 1.0) * centre
            else:
                k_ref[p, k] = pair_weight(weighted, here, dy, dz, scale_of(dy, dz, 0))
        for k, (dy, dz) in enumerate(BESIDE):
            k_ref[p, len(OWN) + k] = pair_weight(weighted, there, dy, dz, scale_of(dy, dz, 1))


def local_kernel(k_ref, orb_ref, *acc_refs):
    base = 0
    for acc_ref in acc_refs:

        @pl.loop(0, acc_ref.shape[0])
        def _(j, acc_ref=acc_ref, base=base):
            for p in range(PLANES):
                groups = {}
                for plane, terms, first in ((p, OWN, 0), (1 - p, BESIDE, len(OWN))):
                    field = orb_ref[base + j, plane]
                    for k, (dy, dz) in enumerate(terms):
                        term = k_ref[p, first + k] * shifted(field, dy, 0)
                        groups[dz] = groups[dz] + term if dz in groups else term
                out = groups[0]
                for dz in (1, -1, 2, -2):
                    out = out + shifted(groups[dz], 0, dz)
                acc_ref[j, p] = out

        base += acc_ref.shape[0]


def nearest():
    odd = lax.rem(lax.axis_index("dom"), 2)
    return odd, 1 - odd


def halo_weight_kernel(hop, orb_count, occ_ref, *refs):
    n = STEPS
    local, slabs, k_ref = refs[:n], refs[n : 2 * n], refs[2 * n]
    weights = block_weights(occ_ref, orb_count)
    near = nearest()[hop]
    far = 1 - near
    pairs = [(r, i) for r in local for i in range(BLOCK)]
    here = [w * r[i, far] for w, (r, i) in zip(weights, pairs)]
    behind = [w * r[i, near] for w, (r, i) in zip(weights, pairs)]
    there = [r[i, near] for r in slabs for i in range(BLOCK)]
    beyond = [r[i, far] for r in slabs for i in range(BLOCK)]
    for k, (dy, dz) in enumerate(BESIDE):
        k_ref[k] = pair_weight(here, there, dy, dz, scale_of(dy, dz, 1))
    k_ref[BEYOND] = pair_weight(here, beyond, 0, 0, TWO)
    k_ref[ACROSS] = pair_weight(behind, there, 0, 0, TWO)


def side_terms(k_ref, near_plane, far_plane):
    groups = {}
    for k, (dy, dz) in enumerate(BESIDE):
        term = k_ref[k] * shifted(near_plane, dy, 0)
        groups[dz] = groups[dz] + term if dz in groups else term
    beside = groups[0] + shifted(groups[1], 0, 1) + shifted(groups[-1], 0, -1)
    return beside + k_ref[BEYOND] * far_plane, k_ref[ACROSS] * near_plane


def finish_kernel(origin, chained, *refs):
    k_refs, acc_ref, refs = refs[:2], refs[2], refs[3:]
    sum_ref, sems = refs[-2:]
    out_ref = refs[-3]
    chunk_refs = refs[: -3 - chained]
    half = len(chunk_refs) // 2
    odd = nearest()[0]
    even = 1 - odd
    base = 0
    for first_ref, second_ref in zip(chunk_refs[:half], chunk_refs[half:]):
        size = first_ref.shape[0] // PLANES

        @pl.loop(0, size, unroll=size)
        def _(i, first_ref=first_ref, second_ref=second_ref, base=base):
            j, at = base + i, PLANES * i
            to_even, to_odd = side_terms(k_refs[0], first_ref[at + odd], first_ref[at + even])
            more_odd, more_even = side_terms(k_refs[1], second_ref[at + even], second_ref[at + odd])
            sum_ref[j, even] = acc_ref[j, even] + (to_even + more_even)
            sum_ref[j, odd] = acc_ref[j, odd] + (to_odd + more_odd)
            pltpu.make_async_copy(sum_ref.at[j], out_ref.at[origin + j], sems.at[j]).start()

        base += size
    for j in range(base):
        pltpu.make_async_copy(sum_ref.at[j], out_ref.at[origin + j], sems.at[j]).wait()


VMEM = pl.BlockSpec(memory_space=pltpu.VMEM)
SMEM = pl.BlockSpec(memory_space=pltpu.SMEM)
ANY = pl.BlockSpec(memory_space=pl.ANY)
PARAMS = pltpu.CompilerParams(vmem_limit_bytes=16 * 1024 * 1024)


def finish(name, origin, weights, acc, chunks, out, shape):
    chained = out is not None
    return pl.pallas_call(
        functools.partial(finish_kernel, origin, chained),
        out_shape=jax.ShapeDtypeStruct(shape, jnp.float32),
        in_specs=[VMEM] * (3 + len(chunks)) + [ANY] * chained,
        out_specs=ANY,
        input_output_aliases={3 + len(chunks): 0} if chained else {},
        scratch_shapes=[pltpu.VMEM(acc.shape, jnp.float32), pltpu.SemaphoreType.DMA((acc.shape[0],))],
        compiler_params=PARAMS,
        cost_estimate=pl.CostEstimate(flops=1, bytes_accessed=1, transcendentals=0),
        name=name,
    )(*weights, acc, *chunks, *([out] if chained else []))


def hops(slabs):
    swap = [(i, i ^ 1) for i in range(slabs)]
    onward = [(i, i + 2 if i % 2 == 0 else i - 2) for i in range(slabs)]
    onward = [(a, b) for a, b in onward if 0 <= b < slabs]
    back = [(b, a) for a, b in onward]
    return swap, onward, back


def everywhere(field, groups):
    band, axis = lax.axis_index("band"), field.ndim - 4
    if groups == STEPS:
        own = lax.dynamic_slice_in_dim(field, band * BLOCK, BLOCK, axis)
        return [own] + [
            lax.ppermute(own, "band", [(i, (i - step) % STEPS) for i in range(STEPS)]) for step in range(1, STEPS)
        ]
    out = []
    for step in range(STEPS):
        mine = lax.slice_in_dim(field, step * BLOCK, (step + 1) * BLOCK, axis=axis)
        mine = jnp.where(band == step * (groups // STEPS), mine, jnp.zeros_like(mine))
        out.append(lax.psum(mine, "band"))
    return out


def after(value, *others):
    return lax.optimization_barrier((value, *others))[0]


def per_device(orbitals, occupations):
    orb_count, planes, rows, columns = orbitals.shape
    groups, slabs = lax.axis_size("band"), lax.axis_size("dom")
    assert planes == PLANES and slabs % 2 == 0 and slabs > 2 and sum(CHUNKS) == orb_count * planes
    swap, onward, back = hops(slabs)
    n = len(CHUNKS)
    starts = [sum(CHUNKS[:i]) for i in range(n)]
    assert all(n % planes == 0 for n in CHUNKS)
    cuts = [0] + [sum(CHUNKS[:upto]) // planes for upto in GROUPS]
    f32 = lambda *shape: jax.ShapeDtypeStruct(shape, jnp.float32)

    sent = pl.pallas_call(
        functools.partial(cut_kernel, starts),
        out_shape=[f32(size, rows, columns) for size in CHUNKS],
        in_specs=[ANY],
        out_specs=[VMEM] * n,
        scratch_shapes=[pltpu.SemaphoreType.DMA((n,))],
        compiler_params=PARAMS,
        name="cut",
    )(orbitals)
    around = lax.ppermute(sent[-1], "dom", back)
    first = [lax.ppermute(part, "dom", swap) for part in sent]
    local = everywhere(orbitals[: STEPS * BLOCK], groups)
    k_local = pl.pallas_call(
        functools.partial(local_weight_kernel, orb_count),
        out_shape=f32(planes, len(OWN) + len(BESIDE), rows, columns),
        in_specs=[SMEM] + [VMEM] * STEPS,
        out_specs=VMEM,
        compiler_params=PARAMS,
        cost_estimate=pl.CostEstimate(flops=1, bytes_accessed=1, transcendentals=0),
        name="local_weights",
    )(occupations, *local)
    acc = pl.pallas_call(
        local_kernel,
        out_shape=[f32(b - a, planes, rows, columns) for a, b in zip(cuts, cuts[1:])],
        in_specs=[VMEM] * 2,
        out_specs=[VMEM] * len(GROUPS),
        compiler_params=PARAMS,
        cost_estimate=pl.CostEstimate(flops=1, bytes_accessed=1, transcendentals=0),
        name="local",
    )(k_local, orbitals)

    count = 0
    while sum(CHUNKS[:count]) < STEPS * BLOCK * planes:
        count += 1

    def halo_weights(name, parts):
        blocks = jnp.concatenate(parts[:count])[: STEPS * BLOCK * planes]
        blocks = everywhere(blocks.reshape(-1, planes, rows, columns), groups)
        return pl.pallas_call(
            functools.partial(halo_weight_kernel, name == "second", orb_count),
            out_shape=f32(ACROSS + 1, rows, columns),
            in_specs=[SMEM] + [VMEM] * (2 * STEPS),
            out_specs=VMEM,
            compiler_params=PARAMS,
            cost_estimate=pl.CostEstimate(flops=1, bytes_accessed=1, transcendentals=0),
            name=name + "_hop_weights",
        )(occupations, *local, *blocks)

    k_first = halo_weights("first", first)
    before = {0: around, 1: k_local, 2: k_first}
    second = [
        lax.ppermute(after(part, before[i]) if i in before else part, "dom", onward) for i, part in enumerate(first[:-1])
    ]
    second.append(lax.ppermute(around, "dom", swap))
    k_halo = [k_first, halo_weights("second", second)]
    acc = [after(acc[0], first[-1]), *acc[1:]]

    out, begin = None, 0
    for g, upto in enumerate(GROUPS):
        chunks = first[begin:upto] + second[begin:upto]
        out = finish(f"finish_{g}", cuts[g], k_halo, acc[g], chunks, out, orbitals.shape)
        begin = upto
    return out


def solution(mesh):
    in_specs = (P("band", "dom", None, None), P())
    out_specs = P("band", "dom", None, None)
    return jax.shard_map(
        per_device, mesh=mesh, in_specs=in_specs, out_specs=out_specs, check_vma=False
    )
```

```python
import functools

import jax
import jax.numpy as jnp
from jax import lax
from jax.experimental import pallas as pl
from jax.experimental.pallas import tpu as pltpu
from jax.sharding import PartitionSpec as P

BLOCK = 2
STEPS = 2
PLANES = 2
CHUNKS = (4, 6, 6, 4, 4)
GROUPS = (3, 5)

ONE = 1.0 / 36.0
TWO = 1.0 / 216.0
CROSS = 2.0 / 216.0

OWN = [(0, 0), (1, 0), (-1, 0), (2, 0), (-2, 0), (0, 1), (1, 1), (-1, 1), (0, -1), (1, -1), (-1, -1), (0, 2), (0, -2)]
BESIDE = [(0, 0), (1, 0), (-1, 0), (0, 1), (0, -1)]
BEYOND, ACROSS = len(BESIDE), len(BESIDE) + 1


def shifted(field, dy, dz):
    rows, columns = field.shape
    if dy:
        field = pltpu.roll(field, (-dy) % rows, 0)
    if dz:
        field = pltpu.roll(field, (-dz) % columns, 1)
    return field


def inside(shape, dy, dz):
    y = lax.broadcasted_iota(jnp.int32, shape, 0) + dy
    z = lax.broadcasted_iota(jnp.int32, shape, 1) - dz
    return (y >= 0) & (y < shape[0]) & (z >= 0) & (z < shape[1])


def pair_weight(here, there, dy, dz, scale):
    total = None
    for h, t in zip(here, there):
        term = shifted(h, 0, -dz) * shifted(t, dy, 0)
        total = term if total is None else total + term
    total = total * (-scale)
    if dy or dz:
        total = jnp.where(inside(total.shape, dy, dz), total, 0.0)
    return total


def scale_of(dy, dz, dx):
    length = abs(dx) + abs(dy) + abs(dz)
    if length == 1:
        return ONE
    return TWO if max(abs(dx), abs(dy), abs(dz)) == 2 else CROSS


def block_weights(occ_ref, orb_count):
    groups = lax.axis_size("band")
    out = []
    for step in range(STEPS):
        s = lax.rem(lax.axis_index("band") + step, STEPS) if groups == STEPS else step
        first = s * (groups // STEPS) * orb_count + s * BLOCK
        out += [occ_ref[first + i] for i in range(BLOCK)]
    return out


def cut_kernel(starts, orb_ref, *refs):
    part_refs, sems = refs[:-1], refs[-1]
    flat = orb_ref.reshape(-1, *orb_ref.shape[2:])
    copies = [
        pltpu.make_async_copy(flat.at[pl.ds(start, part.shape[0])], part, sems.at[i])
        for i, (start, part) in enumerate(zip(starts, part_refs))
    ]
    for copy in copies:
        copy.start()
    for copy in copies:
        copy.wait()


def local_weight_kernel(orb_count, occ_ref, *refs):
    block_refs, k_ref = refs[:STEPS], refs[STEPS]
    rows, columns = k_ref.shape[2:]
    weights = block_weights(occ_ref, orb_count)
    dom, slabs = lax.axis_index("dom"), lax.axis_size("dom")
    for p in range(PLANES):
        here = [r[i, p] for r in block_refs for i in range(BLOCK)]
        there = [r[i, 1 - p] for r in block_refs for i in range(BLOCK)]
        weighted = [w * h for w, h in zip(weights, here)]
        outer = jnp.where(dom == (0 if p == 0 else slabs - 1), 0.0, 1.0)
        y = lax.broadcasted_iota(jnp.int32, (rows, columns), 0)
        z = lax.broadcasted_iota(jnp.int32, (rows, columns), 1)
        edges = (y > 0).astype(jnp.float32) + (y < rows - 1).astype(jnp.float32)
        edges = edges + (z > 0).astype(jnp.float32) + (z < columns - 1).astype(jnp.float32)
        centre = 1.0 / 6.0 + (edges + (1.0 + outer)) * TWO
        for k, (dy, dz) in enumerate(OWN):
            if k == 0:
                k_ref[p, k] = pair_weight(weighted, here, 0, 0, 1.0) * centre
            else:
                k_ref[p, k] = pair_weight(weighted, here, dy, dz, scale_of(dy, dz, 0))
        for k, (dy, dz) in enumerate(BESIDE):
            k_ref[p, len(OWN) + k] = pair_weight(weighted, there, dy, dz, scale_of(dy, dz, 1))


def local_kernel(first, k_ref, orb_ref, acc_ref):
    @pl.loop(0, acc_ref.shape[0])
    def _(j):
        for p in range(PLANES):
            groups = {}
            for plane, terms, base in ((p, OWN, 0), (1 - p, BESIDE, len(OWN))):
                field = orb_ref[first + j, plane]
                for k, (dy, dz) in enumerate(terms):
                    term = k_ref[p, base + k] * shifted(field, dy, 0)
                    groups[dz] = groups[dz] + term if dz in groups else term
            out = groups[0]
            for dz in (1, -1, 2, -2):
                out = out + shifted(groups[dz], 0, dz)
            acc_ref[j, p] = out


def nearest():
    odd = lax.rem(lax.axis_index("dom"), 2)
    return odd, 1 - odd


def halo_weight_kernel(hop, orb_count, occ_ref, *refs):
    n = STEPS
    local, slabs, k_ref = refs[:n], refs[n : 2 * n], refs[2 * n]
    weights = block_weights(occ_ref, orb_count)
    dom, count = lax.axis_index("dom"), lax.axis_size("dom")
    real = jnp.where((dom == 0) | (dom == count - 1), 0.0, 1.0) if hop else 1.0
    near = nearest()[hop]
    far = 1 - near
    pairs = [(r, i) for r in local for i in range(BLOCK)]
    here = [w * r[i, far] for w, (r, i) in zip(weights, pairs)]
    behind = [w * r[i, near] for w, (r, i) in zip(weights, pairs)]
    there = [r[i, near] for r in slabs for i in range(BLOCK)]
    beyond = [r[i, far] for r in slabs for i in range(BLOCK)]
    for k, (dy, dz) in enumerate(BESIDE):
        k_ref[k] = pair_weight(here, there, dy, dz, scale_of(dy, dz, 1) * real)
    k_ref[BEYOND] = pair_weight(here, beyond, 0, 0, TWO * real)
    k_ref[ACROSS] = pair_weight(behind, there, 0, 0, TWO * real)


def side_terms(k_ref, near_plane, far_plane):
    groups = {}
    for k, (dy, dz) in enumerate(BESIDE):
        term = k_ref[k] * shifted(near_plane, dy, 0)
        groups[dz] = groups[dz] + term if dz in groups else term
    beside = groups[0] + shifted(groups[1], 0, 1) + shifted(groups[-1], 0, -1)
    return beside + k_ref[BEYOND] * far_plane, k_ref[ACROSS] * near_plane


def finish_kernel(origin, chained, *refs):
    k_refs, acc_ref, refs = refs[:2], refs[2], refs[3:]
    sum_ref, sems = refs[-2:]
    out_ref = refs[-3]
    chunk_refs = refs[: -3 - chained]
    half = len(chunk_refs) // 2
    odd = nearest()[0]
    even = 1 - odd
    base = 0
    for first_ref, second_ref in zip(chunk_refs[:half], chunk_refs[half:]):
        size = first_ref.shape[0] // PLANES

        @pl.loop(0, size, unroll=size)
        def _(i, first_ref=first_ref, second_ref=second_ref, base=base):
            j, at = base + i, PLANES * i
            to_even, to_odd = side_terms(k_refs[0], first_ref[at + odd], first_ref[at + even])
            more_odd, more_even = side_terms(k_refs[1], second_ref[at + even], second_ref[at + odd])
            sum_ref[j, even] = acc_ref[j, even] + (to_even + more_even)
            sum_ref[j, odd] = acc_ref[j, odd] + (to_odd + more_odd)
            pltpu.make_async_copy(sum_ref.at[j], out_ref.at[origin + j], sems.at[j]).start()

        base += size
    for j in range(base):
        pltpu.make_async_copy(sum_ref.at[j], out_ref.at[origin + j], sems.at[j]).wait()


VMEM = pl.BlockSpec(memory_space=pltpu.VMEM)
SMEM = pl.BlockSpec(memory_space=pltpu.SMEM)
ANY = pl.BlockSpec(memory_space=pl.ANY)
PARAMS = pltpu.CompilerParams(vmem_limit_bytes=16 * 1024 * 1024)


def finish(name, origin, weights, acc, chunks, out, shape):
    chained = out is not None
    return pl.pallas_call(
        functools.partial(finish_kernel, origin, chained),
        out_shape=jax.ShapeDtypeStruct(shape, jnp.float32),
        in_specs=[VMEM] * (3 + len(chunks)) + [ANY] * chained,
        out_specs=ANY,
        input_output_aliases={3 + len(chunks): 0} if chained else {},
        scratch_shapes=[pltpu.VMEM(acc.shape, jnp.float32), pltpu.SemaphoreType.DMA((acc.shape[0],))],
        compiler_params=PARAMS,
        cost_estimate=pl.CostEstimate(flops=1, bytes_accessed=1, transcendentals=0),
        name=name,
    )(*weights, acc, *chunks, *([out] if chained else []))


def hops(slabs):
    swap = [(i, i ^ 1) for i in range(slabs)]
    onward = [(i, i + 2 if i % 2 == 0 else i - 2) for i in range(slabs)]
    ring = [(a, b % slabs) for a, b in onward]
    onward = [(a, b) for a, b in onward if 0 <= b < slabs]
    back = [(b, a) for a, b in onward]
    return swap, onward, ring, back


def everywhere(field, groups):
    band, axis = lax.axis_index("band"), field.ndim - 4
    if groups == STEPS:
        own = lax.dynamic_slice_in_dim(field, band * BLOCK, BLOCK, axis)
        return [own] + [
            lax.ppermute(own, "band", [(i, (i - step) % STEPS) for i in range(STEPS)]) for step in range(1, STEPS)
        ]
    out = []
    for step in range(STEPS):
        mine = lax.slice_in_dim(field, step * BLOCK, (step + 1) * BLOCK, axis=axis)
        mine = jnp.where(band == step * (groups // STEPS), mine, jnp.zeros_like(mine))
        out.append(lax.psum(mine, "band"))
    return out


def after(value, *others):
    return lax.optimization_barrier((value, *others))[0]


def per_device(orbitals, occupations):
    orb_count, planes, rows, columns = orbitals.shape
    groups, slabs = lax.axis_size("band"), lax.axis_size("dom")
    assert planes == PLANES and slabs % 2 == 0 and slabs > 2 and sum(CHUNKS) == orb_count * planes
    swap, onward, ring, back = hops(slabs)
    n = len(CHUNKS)
    starts = [sum(CHUNKS[:i]) for i in range(n)]
    assert all(n % planes == 0 for n in CHUNKS)
    cuts = [0] + [sum(CHUNKS[:upto]) // planes for upto in GROUPS]
    f32 = lambda *shape: jax.ShapeDtypeStruct(shape, jnp.float32)

    def cut(name, ids):
        return pl.pallas_call(
            functools.partial(cut_kernel, [starts[i] for i in ids]),
            out_shape=[f32(CHUNKS[i], rows, columns) for i in ids],
            in_specs=[ANY],
            out_specs=[VMEM] * len(ids),
            scratch_shapes=[pltpu.SemaphoreType.DMA((len(ids),))],
            compiler_params=PARAMS,
            name=name,
        )(orbitals)

    sent = [*cut("cut_first", range(2)), *cut("cut_rest", range(2, n))]
    around = lax.ppermute(sent[-1], "dom", back)
    first = [lax.ppermute(part, "dom", swap) for part in sent]
    local = everywhere(orbitals[: STEPS * BLOCK], groups)
    k_local = pl.pallas_call(
        functools.partial(local_weight_kernel, orb_count),
        out_shape=f32(planes, len(OWN) + len(BESIDE), rows, columns),
        in_specs=[SMEM] + [VMEM] * STEPS,
        out_specs=VMEM,
        compiler_params=PARAMS,
        cost_estimate=pl.CostEstimate(flops=1, bytes_accessed=1, transcendentals=0),
        name="local_weights",
    )(occupations, *local)
    def local_sums(g):
        return pl.pallas_call(
            functools.partial(local_kernel, cuts[g]),
            out_shape=f32(cuts[g + 1] - cuts[g], planes, rows, columns),
            in_specs=[VMEM] * 2,
            out_specs=VMEM,
            compiler_params=PARAMS,
            cost_estimate=pl.CostEstimate(flops=1, bytes_accessed=1, transcendentals=0),
            name=f"local_{g}",
        )(k_local, orbitals)

    acc = [local_sums(g) for g in range(len(GROUPS))]

    count = 0
    while sum(CHUNKS[:count]) < STEPS * BLOCK * planes:
        count += 1

    def halo_weights(name, parts):
        blocks = jnp.concatenate(parts[:count])[: STEPS * BLOCK * planes]
        blocks = everywhere(blocks.reshape(-1, planes, rows, columns), groups)
        return pl.pallas_call(
            functools.partial(halo_weight_kernel, name == "second", orb_count),
            out_shape=f32(ACROSS + 1, rows, columns),
            in_specs=[SMEM] + [VMEM] * (2 * STEPS),
            out_specs=VMEM,
            compiler_params=PARAMS,
            cost_estimate=pl.CostEstimate(flops=1, bytes_accessed=1, transcendentals=0),
            name=name + "_hop_weights",
        )(occupations, *local, *blocks)

    k_first = halo_weights("first", first)
    before = {0: around, 1: k_local, 2: k_first}
    second = [
        lax.ppermute(after(part, before[i]) if i in before else part, "dom", ring if i < n - 2 else onward)
        for i, part in enumerate(first[:-1])
    ]
    second.append(lax.ppermute(around, "dom", swap))
    k_halo = [k_first, halo_weights("second", second)]
    acc = [after(acc[0], first[-1]), *acc[1:]]

    out, begin = None, 0
    for g, upto in enumerate(GROUPS):
        chunks = first[begin:upto] + second[begin:upto]
        out = finish(f"finish_{g}", cuts[g], k_halo, acc[g], chunks, out, orbitals.shape)
        begin = upto
    return out


def solution(mesh):
    in_specs = (P("band", "dom", None, None), P())
    out_specs = P("band", "dom", None, None)
    return jax.shard_map(
        per_device, mesh=mesh, in_specs=in_specs, out_specs=out_specs, check_vma=False
    )
```

```python
import functools

import jax
import jax.numpy as jnp
from jax import lax
from jax.experimental import pallas as pl
from jax.experimental.pallas import tpu as pltpu
from jax.sharding import PartitionSpec as P

BLOCK = 2
STEPS = 2
PLANES = 2
CHUNKS = (4, 6, 6, 4, 4)
GROUPS = (3, 5)

ONE = 1.0 / 36.0
TWO = 1.0 / 216.0
CROSS = 2.0 / 216.0

OWN = [(0, 0), (1, 0), (-1, 0), (2, 0), (-2, 0), (0, 1), (1, 1), (-1, 1), (0, -1), (1, -1), (-1, -1), (0, 2), (0, -2)]
BESIDE = [(0, 0), (1, 0), (-1, 0), (0, 1), (0, -1)]
BEYOND, ACROSS = len(BESIDE), len(BESIDE) + 1


def shifted(field, dy, dz):
    rows, columns = field.shape
    if dy:
        field = pltpu.roll(field, (-dy) % rows, 0)
    if dz:
        field = pltpu.roll(field, (-dz) % columns, 1)
    return field


def inside(shape, dy, dz):
    y = lax.broadcasted_iota(jnp.int32, shape, 0) + dy
    z = lax.broadcasted_iota(jnp.int32, shape, 1) - dz
    return (y >= 0) & (y < shape[0]) & (z >= 0) & (z < shape[1])


def pair_weight(here, there, dy, dz, scale):
    total = None
    for h, t in zip(here, there):
        term = shifted(h, 0, -dz) * shifted(t, dy, 0)
        total = term if total is None else total + term
    total = total * (-scale)
    if dy or dz:
        total = jnp.where(inside(total.shape, dy, dz), total, 0.0)
    return total


def scale_of(dy, dz, dx):
    length = abs(dx) + abs(dy) + abs(dz)
    if length == 1:
        return ONE
    return TWO if max(abs(dx), abs(dy), abs(dz)) == 2 else CROSS


def block_weights(occ_ref, orb_count):
    groups = lax.axis_size("band")
    out = []
    for step in range(STEPS):
        s = lax.rem(lax.axis_index("band") + step, STEPS) if groups == STEPS else step
        first = s * (groups // STEPS) * orb_count + s * BLOCK
        out += [occ_ref[first + i] for i in range(BLOCK)]
    return out


def cut_kernel(starts, orb_ref, *refs):
    part_refs, sems = refs[:-1], refs[-1]
    flat = orb_ref.reshape(-1, *orb_ref.shape[2:])
    copies = [
        pltpu.make_async_copy(flat.at[pl.ds(start, part.shape[0])], part, sems.at[i])
        for i, (start, part) in enumerate(zip(starts, part_refs))
    ]
    for copy in copies:
        copy.start()
    for copy in copies:
        copy.wait()


def local_weight_kernel(orb_count, occ_ref, *refs):
    block_refs, k_ref = refs[:STEPS], refs[STEPS]
    rows, columns = k_ref.shape[2:]
    weights = block_weights(occ_ref, orb_count)
    dom, slabs = lax.axis_index("dom"), lax.axis_size("dom")
    for p in range(PLANES):
        here = [r[i, p] for r in block_refs for i in range(BLOCK)]
        there = [r[i, 1 - p] for r in block_refs for i in range(BLOCK)]
        weighted = [w * h for w, h in zip(weights, here)]
        outer = jnp.where(dom == (0 if p == 0 else slabs - 1), 0.0, 1.0)
        y = lax.broadcasted_iota(jnp.int32, (rows, columns), 0)
        z = lax.broadcasted_iota(jnp.int32, (rows, columns), 1)
        edges = (y > 0).astype(jnp.float32) + (y < rows - 1).astype(jnp.float32)
        edges = edges + (z > 0).astype(jnp.float32) + (z < columns - 1).astype(jnp.float32)
        centre = 1.0 / 6.0 + (edges + (1.0 + outer)) * TWO
        for k, (dy, dz) in enumerate(OWN):
            if k == 0:
                k_ref[p, k] = pair_weight(weighted, here, 0, 0, 1.0) * centre
            else:
                k_ref[p, k] = pair_weight(weighted, here, dy, dz, scale_of(dy, dz, 0))
        for k, (dy, dz) in enumerate(BESIDE):
            k_ref[p, len(OWN) + k] = pair_weight(weighted, there, dy, dz, scale_of(dy, dz, 1))


def local_kernel(first, k_ref, orb_ref, acc_ref):
    @pl.loop(0, acc_ref.shape[0])
    def _(j):
        for p in range(PLANES):
            groups = {}
            for plane, terms, base in ((p, OWN, 0), (1 - p, BESIDE, len(OWN))):
                field = orb_ref[first + j, plane]
                for k, (dy, dz) in enumerate(terms):
                    term = k_ref[p, base + k] * shifted(field, dy, 0)
                    groups[dz] = groups[dz] + term if dz in groups else term
            out = groups[0]
            for dz in (1, -1, 2, -2):
                out = out + shifted(groups[dz], 0, dz)
            acc_ref[j, p] = out


def nearest():
    odd = lax.rem(lax.axis_index("dom"), 2)
    return odd, 1 - odd


def halo_weight_kernel(hop, orb_count, occ_ref, *refs):
    n = STEPS
    local, slabs, k_ref = refs[:n], refs[n : 2 * n], refs[2 * n]
    weights = block_weights(occ_ref, orb_count)
    dom, count = lax.axis_index("dom"), lax.axis_size("dom")
    real = jnp.where((dom == 0) | (dom == count - 1), 0.0, 1.0) if hop else 1.0
    near = nearest()[hop]
    far = 1 - near
    pairs = [(r, i) for r in local for i in range(BLOCK)]
    here = [w * r[i, far] for w, (r, i) in zip(weights, pairs)]
    behind = [w * r[i, near] for w, (r, i) in zip(weights, pairs)]
    there = [r[i, near] for r in slabs for i in range(BLOCK)]
    beyond = [r[i, far] for r in slabs for i in range(BLOCK)]
    for k, (dy, dz) in enumerate(BESIDE):
        k_ref[k] = pair_weight(here, there, dy, dz, scale_of(dy, dz, 1) * real)
    k_ref[BEYOND] = pair_weight(here, beyond, 0, 0, TWO * real)
    k_ref[ACROSS] = pair_weight(behind, there, 0, 0, TWO * real)


def side_terms(k_ref, near_plane, far_plane):
    groups = {}
    for k, (dy, dz) in enumerate(BESIDE):
        term = k_ref[k] * shifted(near_plane, dy, 0)
        groups[dz] = groups[dz] + term if dz in groups else term
    beside = groups[0] + shifted(groups[1], 0, 1) + shifted(groups[-1], 0, -1)
    return beside + k_ref[BEYOND] * far_plane, k_ref[ACROSS] * near_plane


def add_first_kernel(k_ref, acc_ref, *refs):
    out_ref = refs[-1]
    odd = nearest()[0]
    even = 1 - odd
    base = 0
    for first_ref in refs[:-1]:
        size = first_ref.shape[0] // PLANES

        @pl.loop(0, size, unroll=size)
        def _(i, first_ref=first_ref, base=base):
            j, at = base + i, PLANES * i
            to_even, to_odd = side_terms(k_ref, first_ref[at + odd], first_ref[at + even])
            out_ref[j, even] = acc_ref[j, even] + to_even
            out_ref[j, odd] = acc_ref[j, odd] + to_odd

        base += size


def finish_kernel(origin, hops_left, chained, *refs):
    k_refs, acc_ref, refs = refs[:2], refs[2], refs[3:]
    sum_ref, sems = refs[-2:]
    out_ref = refs[-3]
    chunk_refs = refs[: -3 - chained]
    count = len(chunk_refs) // hops_left
    odd = nearest()[0]
    even = 1 - odd
    base = 0
    for at_chunk in range(count):
        second_ref = chunk_refs[-count:][at_chunk]
        first_ref = chunk_refs[at_chunk]
        size = second_ref.shape[0] // PLANES

        @pl.loop(0, size, unroll=size)
        def _(i, first_ref=first_ref, second_ref=second_ref, base=base):
            j, at = base + i, PLANES * i
            to_odd, to_even = side_terms(k_refs[1], second_ref[at + even], second_ref[at + odd])
            if hops_left == 2:
                more_even, more_odd = side_terms(k_refs[0], first_ref[at + odd], first_ref[at + even])
                to_even, to_odd = to_even + more_even, to_odd + more_odd
            sum_ref[j, even] = acc_ref[j, even] + to_even
            sum_ref[j, odd] = acc_ref[j, odd] + to_odd
            pltpu.make_async_copy(sum_ref.at[j], out_ref.at[origin + j], sems.at[j]).start()

        base += size
    for j in range(base):
        pltpu.make_async_copy(sum_ref.at[j], out_ref.at[origin + j], sems.at[j]).wait()


VMEM = pl.BlockSpec(memory_space=pltpu.VMEM)
SMEM = pl.BlockSpec(memory_space=pltpu.SMEM)
ANY = pl.BlockSpec(memory_space=pl.ANY)
PARAMS = pltpu.CompilerParams(vmem_limit_bytes=16 * 1024 * 1024)


def finish(name, origin, hops_left, weights, acc, chunks, out, shape):
    chained = out is not None
    return pl.pallas_call(
        functools.partial(finish_kernel, origin, hops_left, chained),
        out_shape=jax.ShapeDtypeStruct(shape, jnp.float32),
        in_specs=[VMEM] * (3 + len(chunks)) + [ANY] * chained,
        out_specs=ANY,
        input_output_aliases={3 + len(chunks): 0} if chained else {},
        scratch_shapes=[pltpu.VMEM(acc.shape, jnp.float32), pltpu.SemaphoreType.DMA((acc.shape[0],))],
        compiler_params=PARAMS,
        cost_estimate=pl.CostEstimate(flops=1, bytes_accessed=1, transcendentals=0),
        name=name,
    )(*weights, acc, *chunks, *([out] if chained else []))


def hops(slabs):
    swap = [(i, i ^ 1) for i in range(slabs)]
    onward = [(i, i + 2 if i % 2 == 0 else i - 2) for i in range(slabs)]
    ring = [(a, b % slabs) for a, b in onward]
    onward = [(a, b) for a, b in onward if 0 <= b < slabs]
    back = [(b, a) for a, b in onward]
    return swap, onward, ring, back


def everywhere(field, groups):
    band, axis = lax.axis_index("band"), field.ndim - 4
    if groups == STEPS:
        own = lax.dynamic_slice_in_dim(field, band * BLOCK, BLOCK, axis)
        return [own] + [
            lax.ppermute(own, "band", [(i, (i - step) % STEPS) for i in range(STEPS)]) for step in range(1, STEPS)
        ]
    out = []
    for step in range(STEPS):
        mine = lax.slice_in_dim(field, step * BLOCK, (step + 1) * BLOCK, axis=axis)
        mine = jnp.where(band == step * (groups // STEPS), mine, jnp.zeros_like(mine))
        out.append(lax.psum(mine, "band"))
    return out


def after(value, *others):
    return lax.optimization_barrier((value, *others))[0]


def per_device(orbitals, occupations):
    orb_count, planes, rows, columns = orbitals.shape
    groups, slabs = lax.axis_size("band"), lax.axis_size("dom")
    assert planes == PLANES and slabs % 2 == 0 and slabs > 2 and sum(CHUNKS) == orb_count * planes
    swap, onward, ring, back = hops(slabs)
    n = len(CHUNKS)
    starts = [sum(CHUNKS[:i]) for i in range(n)]
    assert all(n % planes == 0 for n in CHUNKS)
    cuts = [0] + [sum(CHUNKS[:upto]) // planes for upto in GROUPS]
    f32 = lambda *shape: jax.ShapeDtypeStruct(shape, jnp.float32)

    def cut(name, ids):
        return pl.pallas_call(
            functools.partial(cut_kernel, [starts[i] for i in ids]),
            out_shape=[f32(CHUNKS[i], rows, columns) for i in ids],
            in_specs=[ANY],
            out_specs=[VMEM] * len(ids),
            scratch_shapes=[pltpu.SemaphoreType.DMA((len(ids),))],
            compiler_params=PARAMS,
            name=name,
        )(orbitals)

    sent = [*cut("cut_first", range(2)), *cut("cut_rest", range(2, n))]
    around = lax.ppermute(sent[-1], "dom", back)
    first = [lax.ppermute(part, "dom", swap) for part in sent]
    local = everywhere(orbitals[: STEPS * BLOCK], groups)
    k_local = pl.pallas_call(
        functools.partial(local_weight_kernel, orb_count),
        out_shape=f32(planes, len(OWN) + len(BESIDE), rows, columns),
        in_specs=[SMEM] + [VMEM] * STEPS,
        out_specs=VMEM,
        compiler_params=PARAMS,
        cost_estimate=pl.CostEstimate(flops=1, bytes_accessed=1, transcendentals=0),
        name="local_weights",
    )(occupations, *local)
    def local_sums(g):
        return pl.pallas_call(
            functools.partial(local_kernel, cuts[g]),
            out_shape=f32(cuts[g + 1] - cuts[g], planes, rows, columns),
            in_specs=[VMEM] * 2,
            out_specs=VMEM,
            compiler_params=PARAMS,
            cost_estimate=pl.CostEstimate(flops=1, bytes_accessed=1, transcendentals=0),
            name=f"local_{g}",
        )(k_local, orbitals)

    acc = [local_sums(g) for g in range(len(GROUPS))]

    count = 0
    while sum(CHUNKS[:count]) < STEPS * BLOCK * planes:
        count += 1

    def halo_weights(name, parts):
        blocks = jnp.concatenate(parts[:count])[: STEPS * BLOCK * planes]
        blocks = everywhere(blocks.reshape(-1, planes, rows, columns), groups)
        return pl.pallas_call(
            functools.partial(halo_weight_kernel, name == "second", orb_count),
            out_shape=f32(ACROSS + 1, rows, columns),
            in_specs=[SMEM] + [VMEM] * (2 * STEPS),
            out_specs=VMEM,
            compiler_params=PARAMS,
            cost_estimate=pl.CostEstimate(flops=1, bytes_accessed=1, transcendentals=0),
            name=name + "_hop_weights",
        )(occupations, *local, *blocks)

    k_first = halo_weights("first", first)
    before = {0: around, 1: k_local, 2: k_first}
    second = [
        lax.ppermute(after(part, before[i]) if i in before else part, "dom", ring if i < n - 2 else onward)
        for i, part in enumerate(first[:-1])
    ]
    second.append(lax.ppermute(around, "dom", swap))
    k_halo = [k_first, halo_weights("second", second)]
    acc = [after(acc[0], first[-1]), *acc[1:]]

    out, begin = None, 0
    for g, upto in enumerate(GROUPS):
        last = g == len(GROUPS) - 1
        chunks = ([] if last else first[begin:upto]) + second[begin:upto]
        if last:
            acc[g] = pl.pallas_call(
                add_first_kernel,
                out_shape=f32(*acc[g].shape),
                in_specs=[VMEM] * (2 + upto - begin),
                out_specs=VMEM,
                compiler_params=PARAMS,
                cost_estimate=pl.CostEstimate(flops=1, bytes_accessed=1, transcendentals=0),
                name="add_first",
            )(k_first, acc[g], *first[begin:upto])
        out = finish(f"finish_{g}", cuts[g], 1 if last else 2, k_halo, acc[g], chunks, out, orbitals.shape)
        begin = upto
    return out


def solution(mesh):
    in_specs = (P("band", "dom", None, None), P())
    out_specs = P("band", "dom", None, None)
    return jax.shard_map(
        per_device, mesh=mesh, in_specs=in_specs, out_specs=out_specs, check_vma=False
    )
```

```python
import functools

import jax
import jax.numpy as jnp
from jax import lax
from jax.experimental import pallas as pl
from jax.experimental.pallas import tpu as pltpu
from jax.sharding import PartitionSpec as P

BLOCK = 2
STEPS = 2
PLANES = 2
CHUNKS = (4, 6, 6, 4, 4)
GROUPS = (3, 5)

ONE = 1.0 / 36.0
TWO = 1.0 / 216.0
CROSS = 2.0 / 216.0

OWN = [(0, 0), (1, 0), (-1, 0), (2, 0), (-2, 0), (0, 1), (1, 1), (-1, 1), (0, -1), (1, -1), (-1, -1), (0, 2), (0, -2)]
BESIDE = [(0, 0), (1, 0), (-1, 0), (0, 1), (0, -1)]
BEYOND, ACROSS = len(BESIDE), len(BESIDE) + 1


def shifted(field, dy, dz):
    rows, columns = field.shape
    if dy:
        field = pltpu.roll(field, (-dy) % rows, 0)
    if dz:
        field = pltpu.roll(field, (-dz) % columns, 1)
    return field


def inside(shape, dy, dz):
    y = lax.broadcasted_iota(jnp.int32, shape, 0) + dy
    z = lax.broadcasted_iota(jnp.int32, shape, 1) - dz
    return (y >= 0) & (y < shape[0]) & (z >= 0) & (z < shape[1])


def pair_weight(here, there, dy, dz, scale):
    total = None
    for h, t in zip(here, there):
        term = shifted(h, 0, -dz) * shifted(t, dy, 0)
        total = term if total is None else total + term
    total = total * (-scale)
    if dy or dz:
        total = jnp.where(inside(total.shape, dy, dz), total, 0.0)
    return total


def scale_of(dy, dz, dx):
    length = abs(dx) + abs(dy) + abs(dz)
    if length == 1:
        return ONE
    return TWO if max(abs(dx), abs(dy), abs(dz)) == 2 else CROSS


def block_weights(occ_ref, orb_count):
    groups = lax.axis_size("band")
    out = []
    for step in range(STEPS):
        s = lax.rem(lax.axis_index("band") + step, STEPS) if groups == STEPS else step
        first = s * (groups // STEPS) * orb_count + s * BLOCK
        out += [occ_ref[first + i] for i in range(BLOCK)]
    return out


def cut_kernel(starts, orb_ref, *refs):
    part_refs, sems = refs[:-1], refs[-1]
    flat = orb_ref.reshape(-1, *orb_ref.shape[2:])
    copies = [
        pltpu.make_async_copy(flat.at[pl.ds(start, part.shape[0])], part, sems.at[i])
        for i, (start, part) in enumerate(zip(starts, part_refs))
    ]
    for copy in copies:
        copy.start()
    for copy in copies:
        copy.wait()


def local_weight_kernel(orb_count, occ_ref, *refs):
    block_refs, k_ref = refs[:STEPS], refs[STEPS]
    rows, columns = k_ref.shape[2:]
    weights = block_weights(occ_ref, orb_count)
    dom, slabs = lax.axis_index("dom"), lax.axis_size("dom")
    for p in range(PLANES):
        here = [r[i, p] for r in block_refs for i in range(BLOCK)]
        there = [r[i, 1 - p] for r in block_refs for i in range(BLOCK)]
        weighted = [w * h for w, h in zip(weights, here)]
        outer = jnp.where(dom == (0 if p == 0 else slabs - 1), 0.0, 1.0)
        y = lax.broadcasted_iota(jnp.int32, (rows, columns), 0)
        z = lax.broadcasted_iota(jnp.int32, (rows, columns), 1)
        edges = (y > 0).astype(jnp.float32) + (y < rows - 1).astype(jnp.float32)
        edges = edges + (z > 0).astype(jnp.float32) + (z < columns - 1).astype(jnp.float32)
        centre = 1.0 / 6.0 + (edges + (1.0 + outer)) * TWO
        for k, (dy, dz) in enumerate(OWN):
            if k == 0:
                k_ref[p, k] = pair_weight(weighted, here, 0, 0, 1.0) * centre
            else:
                k_ref[p, k] = pair_weight(weighted, here, dy, dz, scale_of(dy, dz, 0))
        for k, (dy, dz) in enumerate(BESIDE):
            k_ref[p, len(OWN) + k] = pair_weight(weighted, there, dy, dz, scale_of(dy, dz, 1))


def local_kernel(first, k_ref, orb_ref, acc_ref):
    @pl.loop(0, acc_ref.shape[0], unroll=2)
    def _(j):
        for p in range(PLANES):
            groups = {}
            for plane, terms, base in ((p, OWN, 0), (1 - p, BESIDE, len(OWN))):
                field = orb_ref[first + j, plane]
                for k, (dy, dz) in enumerate(terms):
                    term = k_ref[p, base + k] * shifted(field, dy, 0)
                    groups[dz] = groups[dz] + term if dz in groups else term
            out = groups[0]
            for dz in (1, -1, 2, -2):
                out = out + shifted(groups[dz], 0, dz)
            acc_ref[j, p] = out


def nearest():
    odd = lax.rem(lax.axis_index("dom"), 2)
    return odd, 1 - odd


def halo_weight_kernel(hop, orb_count, occ_ref, *refs):
    n = STEPS
    local, slabs, k_ref = refs[:n], refs[n : 2 * n], refs[2 * n]
    weights = block_weights(occ_ref, orb_count)
    dom, count = lax.axis_index("dom"), lax.axis_size("dom")
    real = jnp.where((dom == 0) | (dom == count - 1), 0.0, 1.0) if hop else 1.0
    near = nearest()[hop]
    far = 1 - near
    pairs = [(r, i) for r in local for i in range(BLOCK)]
    here = [w * r[i, far] for w, (r, i) in zip(weights, pairs)]
    behind = [w * r[i, near] for w, (r, i) in zip(weights, pairs)]
    there = [r[i, near] for r in slabs for i in range(BLOCK)]
    beyond = [r[i, far] for r in slabs for i in range(BLOCK)]
    for k, (dy, dz) in enumerate(BESIDE):
        k_ref[k] = pair_weight(here, there, dy, dz, scale_of(dy, dz, 1) * real)
    k_ref[BEYOND] = pair_weight(here, beyond, 0, 0, TWO * real)
    k_ref[ACROSS] = pair_weight(behind, there, 0, 0, TWO * real)


def side_terms(k_ref, near_plane, far_plane):
    groups = {}
    for k, (dy, dz) in enumerate(BESIDE):
        term = k_ref[k] * shifted(near_plane, dy, 0)
        groups[dz] = groups[dz] + term if dz in groups else term
    beside = groups[0] + shifted(groups[1], 0, 1) + shifted(groups[-1], 0, -1)
    return beside + k_ref[BEYOND] * far_plane, k_ref[ACROSS] * near_plane


def add_first_kernel(k_ref, acc_ref, *refs):
    out_ref = refs[-1]
    odd = nearest()[0]
    even = 1 - odd
    base = 0
    for first_ref in refs[:-1]:
        size = first_ref.shape[0] // PLANES

        @pl.loop(0, size, unroll=size)
        def _(i, first_ref=first_ref, base=base):
            j, at = base + i, PLANES * i
            to_even, to_odd = side_terms(k_ref, first_ref[at + odd], first_ref[at + even])
            out_ref[j, even] = acc_ref[j, even] + to_even
            out_ref[j, odd] = acc_ref[j, odd] + to_odd

        base += size


def finish_kernel(origin, hops_left, chained, *refs):
    k_refs, acc_ref, refs = refs[:2], refs[2], refs[3:]
    sum_ref, sems = refs[-2:]
    out_ref = refs[-3]
    chunk_refs = refs[: -3 - chained]
    count = len(chunk_refs) // hops_left
    odd = nearest()[0]
    even = 1 - odd
    base = 0
    for at_chunk in range(count):
        second_ref = chunk_refs[-count:][at_chunk]
        first_ref = chunk_refs[at_chunk]
        size = second_ref.shape[0] // PLANES

        @pl.loop(0, size, unroll=size)
        def _(i, first_ref=first_ref, second_ref=second_ref, base=base):
            j, at = base + i, PLANES * i
            to_odd, to_even = side_terms(k_refs[1], second_ref[at + even], second_ref[at + odd])
            if hops_left == 2:
                more_even, more_odd = side_terms(k_refs[0], first_ref[at + odd], first_ref[at + even])
                to_even, to_odd = to_even + more_even, to_odd + more_odd
            sum_ref[j, even] = acc_ref[j, even] + to_even
            sum_ref[j, odd] = acc_ref[j, odd] + to_odd
            pltpu.make_async_copy(sum_ref.at[j], out_ref.at[origin + j], sems.at[j]).start()

        base += size
    for j in range(base):
        pltpu.make_async_copy(sum_ref.at[j], out_ref.at[origin + j], sems.at[j]).wait()


VMEM = pl.BlockSpec(memory_space=pltpu.VMEM)
SMEM = pl.BlockSpec(memory_space=pltpu.SMEM)
ANY = pl.BlockSpec(memory_space=pl.ANY)
PARAMS = pltpu.CompilerParams(vmem_limit_bytes=16 * 1024 * 1024)


def finish(name, origin, hops_left, weights, acc, chunks, out, shape):
    chained = out is not None
    return pl.pallas_call(
        functools.partial(finish_kernel, origin, hops_left, chained),
        out_shape=jax.ShapeDtypeStruct(shape, jnp.float32),
        in_specs=[VMEM] * (3 + len(chunks)) + [ANY] * chained,
        out_specs=ANY,
        input_output_aliases={3 + len(chunks): 0} if chained else {},
        scratch_shapes=[pltpu.VMEM(acc.shape, jnp.float32), pltpu.SemaphoreType.DMA((acc.shape[0],))],
        compiler_params=PARAMS,
        cost_estimate=pl.CostEstimate(flops=1, bytes_accessed=1, transcendentals=0),
        name=name,
    )(*weights, acc, *chunks, *([out] if chained else []))


def hops(slabs):
    swap = [(i, i ^ 1) for i in range(slabs)]
    onward = [(i, i + 2 if i % 2 == 0 else i - 2) for i in range(slabs)]
    ring = [(a, b % slabs) for a, b in onward]
    onward = [(a, b) for a, b in onward if 0 <= b < slabs]
    back = [(b, a) for a, b in onward]
    return swap, onward, ring, back


def everywhere(field, groups):
    band, axis = lax.axis_index("band"), field.ndim - 4
    if groups == STEPS:
        own = lax.dynamic_slice_in_dim(field, band * BLOCK, BLOCK, axis)
        return [own] + [
            lax.ppermute(own, "band", [(i, (i - step) % STEPS) for i in range(STEPS)]) for step in range(1, STEPS)
        ]
    out = []
    for step in range(STEPS):
        mine = lax.slice_in_dim(field, step * BLOCK, (step + 1) * BLOCK, axis=axis)
        mine = jnp.where(band == step * (groups // STEPS), mine, jnp.zeros_like(mine))
        out.append(lax.psum(mine, "band"))
    return out


def after(value, *others):
    return lax.optimization_barrier((value, *others))[0]


def per_device(orbitals, occupations):
    orb_count, planes, rows, columns = orbitals.shape
    groups, slabs = lax.axis_size("band"), lax.axis_size("dom")
    assert planes == PLANES and slabs % 2 == 0 and slabs > 2 and sum(CHUNKS) == orb_count * planes
    swap, onward, ring, back = hops(slabs)
    n = len(CHUNKS)
    starts = [sum(CHUNKS[:i]) for i in range(n)]
    assert all(n % planes == 0 for n in CHUNKS)
    cuts = [0] + [sum(CHUNKS[:upto]) // planes for upto in GROUPS]
    f32 = lambda *shape: jax.ShapeDtypeStruct(shape, jnp.float32)

    def cut(name, ids):
        return pl.pallas_call(
            functools.partial(cut_kernel, [starts[i] for i in ids]),
            out_shape=[f32(CHUNKS[i], rows, columns) for i in ids],
            in_specs=[ANY],
            out_specs=[VMEM] * len(ids),
            scratch_shapes=[pltpu.SemaphoreType.DMA((len(ids),))],
            compiler_params=PARAMS,
            name=name,
        )(orbitals)

    sent = [*cut("cut_first", range(2)), *cut("cut_rest", range(2, n))]
    around = lax.ppermute(sent[-1], "dom", back)
    first = [lax.ppermute(part, "dom", swap) for part in sent]
    local = everywhere(orbitals[: STEPS * BLOCK], groups)
    k_local = pl.pallas_call(
        functools.partial(local_weight_kernel, orb_count),
        out_shape=f32(planes, len(OWN) + len(BESIDE), rows, columns),
        in_specs=[SMEM] + [VMEM] * STEPS,
        out_specs=VMEM,
        compiler_params=PARAMS,
        cost_estimate=pl.CostEstimate(flops=1, bytes_accessed=1, transcendentals=0),
        name="local_weights",
    )(occupations, *local)
    def local_sums(g):
        return pl.pallas_call(
            functools.partial(local_kernel, cuts[g]),
            out_shape=f32(cuts[g + 1] - cuts[g], planes, rows, columns),
            in_specs=[VMEM] * 2,
            out_specs=VMEM,
            compiler_params=PARAMS,
            cost_estimate=pl.CostEstimate(flops=1, bytes_accessed=1, transcendentals=0),
            name=f"local_{g}",
        )(k_local, orbitals)

    acc = [local_sums(g) for g in range(len(GROUPS))]

    count = 0
    while sum(CHUNKS[:count]) < STEPS * BLOCK * planes:
        count += 1

    def halo_weights(name, parts):
        blocks = jnp.concatenate(parts[:count])[: STEPS * BLOCK * planes]
        blocks = everywhere(blocks.reshape(-1, planes, rows, columns), groups)
        return pl.pallas_call(
            functools.partial(halo_weight_kernel, name == "second", orb_count),
            out_shape=f32(ACROSS + 1, rows, columns),
            in_specs=[SMEM] + [VMEM] * (2 * STEPS),
            out_specs=VMEM,
            compiler_params=PARAMS,
            cost_estimate=pl.CostEstimate(flops=1, bytes_accessed=1, transcendentals=0),
            name=name + "_hop_weights",
        )(occupations, *local, *blocks)

    k_first = halo_weights("first", first)
    before = {0: around, 1: k_local, 2: k_first}
    second = [
        lax.ppermute(after(part, before[i]) if i in before else part, "dom", ring if i < n - 2 else onward)
        for i, part in enumerate(first[:-1])
    ]
    second.append(lax.ppermute(around, "dom", swap))
    k_halo = [k_first, halo_weights("second", second)]
    acc = [after(acc[0], first[-1]), *acc[1:]]

    out, begin = None, 0
    for g, upto in enumerate(GROUPS):
        last = g == len(GROUPS) - 1
        chunks = ([] if last else first[begin:upto]) + second[begin:upto]
        if last:
            acc[g] = pl.pallas_call(
                add_first_kernel,
                out_shape=f32(*acc[g].shape),
                in_specs=[VMEM] * (2 + upto - begin),
                out_specs=VMEM,
                compiler_params=PARAMS,
                cost_estimate=pl.CostEstimate(flops=1, bytes_accessed=1, transcendentals=0),
                name="add_first",
            )(k_first, acc[g], *first[begin:upto])
        out = finish(f"finish_{g}", cuts[g], 1 if last else 2, k_halo, acc[g], chunks, out, orbitals.shape)
        begin = upto
    return out


def solution(mesh):
    in_specs = (P("band", "dom", None, None), P())
    out_specs = P("band", "dom", None, None)
    return jax.shard_map(
        per_device, mesh=mesh, in_specs=in_specs, out_specs=out_specs, check_vma=False
    )
```
